32 devices in a mesh: ao: 4 (over z), mo: 8 (over y, x, core).
Axes of the slice: x: 2, y: 2, z: 4, core: 2. Of those that a mesh axis runs over, the one named last changes fastest.
Arguments:
- pair_ints: bfloat16 [32, 4096, 256], P(('ao', 'mo')), may hold values from -6 to 6
- shell_pairs: int32 [32, 2], replicated, may hold values from 0 to 31, as said below
- occ_lam: bfloat16 [16, 32], replicated, may hold values from -1.5 to 1.5
- occ_sig: bfloat16 [16, 4], replicated, may hold values from -1.5 to 1.5
- coef_act: bfloat16 [2048, 2048], P(None, 'mo'), may hold values from -0.1875 to 0.1875
- slabs: int32 [2], replicated, may hold values from 0 to 7, as said below
Outputs:
- mo_ints: bfloat16 [2, 4, 4, 2048, 2048], P(None, 'ao', None, 'mo')
The draws below stay inside these ranges and needn't reach their ends.
Inputs may be any that keep to these rules, and one draw needn't show every extreme that they name: `shell_pairs`: each row holds two shell numbers P <= Q, no two rows are equal, and some row holds 0 and 31. `slabs`: the two slab numbers differ.
All inputs are finite; a program needn't handle non-finite values.
Results may differ from the reference program's by a relative error of at most 0.0066.
Values may be sent and summed in bfloat16 or wider, within the bound.
A program may use at most 128 MiB of HBM per device.

```python
import jax
import jax.numpy as jnp
from jax import lax

SH = 64
NSH = 32
NAO = 2048
ACT = 2048
KL = 16
KS = 16
NI = 4
NSLAB = 8
NOCC = 32
NJ = 4
NBLK = 32


def draw_shell_pairs(key, part):
    first_shell, second_shell = jnp.triu_indices(NSH)
    pair_count = NSH * (NSH + 1) // 2
    corner_index = NSH - 1
    shuffled = jax.random.permutation(jax.random.fold_in(key, 11), pair_count - 1).astype(jnp.int32)
    shuffled = jnp.where(shuffled >= corner_index, shuffled + 1, shuffled)
    chosen = jnp.concatenate([jnp.full((1,), corner_index, jnp.int32), shuffled[:NBLK - 1]])
    reorder = jax.random.permutation(jax.random.fold_in(key, 12), NBLK)
    chosen = chosen[reorder]
    shell_one = jnp.asarray(first_shell, jnp.int32)[chosen]
    shell_two = jnp.asarray(second_shell, jnp.int32)[chosen]
    return jnp.stack([shell_one, shell_two], axis=1).astype(jnp.int32)


def draw_slabs(key, part):
    other_slab = jax.random.randint(jax.random.fold_in(key, 21), (), 0, NSLAB - 1).astype(jnp.int32)
    flipped = jax.random.randint(jax.random.fold_in(key, 22), (), 0, 2).astype(jnp.int32)
    last_slab = jnp.full((), NSLAB - 1, jnp.int32)
    first_value = jnp.where(flipped == 0, other_slab, last_slab)
    second_value = jnp.where(flipped == 0, last_slab, other_slab)
    return jnp.stack([first_value, second_value]).astype(jnp.int32)


def block_scale(rng, dims, cuts, least, largest):
    gain = 1.0
    for dim, blocks in cuts:
        draws = jax.random.uniform(jax.random.fold_in(jax.random.fold_in(rng, 6), dim), (blocks,), jnp.float32, least / len(cuts), largest / len(cuts))
        gain = gain * jnp.repeat(jnp.exp(draws), dims[dim] // blocks).reshape((-1,) + (1,) * (len(dims) - 1 - dim))
    return gain


def gaussian(key, dims, scale, bound, shards=(), held_as=jnp.bfloat16):
    result = scale * jax.random.normal(key, dims, jnp.float32)
    if shards:
        result = result * block_scale(key, dims, shards, -0.22, 0.18)
    return jnp.clip(result, -bound, bound).astype(held_as)


def setup_inputs(seed: int = 0) -> dict:
    keys = jax.random.split(jax.random.key(seed), 7)
    pair_ints = gaussian(keys[0], (NBLK, SH * SH, KL * KS), 1.0, 6.0, ((0, 32),))
    shell_pairs = draw_shell_pairs(jax.random.fold_in(keys[6], 71), 0)
    occ_lam = gaussian(keys[2], (KL, NOCC), KL ** -0.5, 1.5)
    occ_sig = gaussian(keys[3], (KS, NJ), KS ** -0.5, 1.5)
    coef_act = gaussian(keys[4], (NAO, ACT), (SH * 16) ** -0.5, 0.1875, ((1, 8),))
    slabs = draw_slabs(jax.random.fold_in(keys[6], 71), 0)
    return dict(pair_ints=pair_ints, shell_pairs=shell_pairs, occ_lam=occ_lam, occ_sig=occ_sig, coef_act=coef_act, slabs=slabs)


def one_slab(pair_ints, shell_pairs, occ_lam, occ_sig, coef_act, slab_index):
    lam_cols = lax.dynamic_slice_in_dim(occ_lam.astype(jnp.float32), slab_index * NI, NI, 1)
    pair_coef = occ_sig.astype(jnp.float32).T[:, None, None, :] * lam_cols.T[None, :, :, None]
    pair_coef = pair_coef.reshape(NJ * NI, KL * KS).astype(jnp.bfloat16)
    half_ints = jnp.dot(pair_ints.reshape(NBLK * SH * SH, KL * KS), pair_coef.T, preferred_element_type=jnp.float32)
    half_ints = half_ints.astype(jnp.bfloat16).reshape(NBLK, SH, SH, NJ, NI)
    per_orbital = jnp.moveaxis(half_ints, 3, 0)
    coef_shells = coef_act.astype(jnp.float32).reshape(NSH, SH, ACT)

    def per_occupied(orbital_blocks):
        def add_block(left_terms, block_item):
            block_vals, block_pair = block_item
            shell_one = block_pair[0]
            shell_two = block_pair[1]
            values = block_vals.astype(jnp.float32)
            term_one = jnp.einsum('mni,ma->ian', values, coef_shells[shell_one])
            differs = (shell_one != shell_two).astype(jnp.float32)
            term_two = jnp.einsum('mni,na->iam', values, coef_shells[shell_two]) * differs
            left_terms = left_terms.at[:, :, shell_two].add(term_one)
            left_terms = left_terms.at[:, :, shell_one].add(term_two)
            return left_terms, None

        start_terms = jnp.zeros((NI, ACT, NSH, SH), jnp.float32)
        left_terms = lax.scan(add_block, start_terms, (orbital_blocks, shell_pairs))[0]
        left_rounded = left_terms.astype(jnp.bfloat16).reshape(NI * ACT, NAO)
        product = jnp.dot(left_rounded, coef_act, preferred_element_type=jnp.float32)
        return product.astype(jnp.bfloat16).reshape(NI, ACT, ACT)

    return lax.map(per_occupied, per_orbital)


def reference(pair_ints, shell_pairs, occ_lam, occ_sig, coef_act, slabs):
    first_slab = one_slab(pair_ints, shell_pairs, occ_lam, occ_sig, coef_act, slabs[0])
    second_slab = one_slab(pair_ints, shell_pairs, occ_lam, occ_sig, coef_act, slabs[1])
    return jnp.stack([first_slab, second_slab])
```

```python
import functools

import jax
import jax.numpy as jnp
from jax import lax
from jax.experimental import pallas as pl
from jax.experimental.pallas import tpu as pltpu
from jax.sharding import PartitionSpec as P

SH = 64
NSH = 32
ACT = 2048
KL = 16
KS = 16
NI = 4
MESH = pl.DeviceIdType.MESH


def pair_coefficients(occ_lam, occ_sig, slab_index):
    nj_all = occ_sig.shape[1]
    lam_cols = lax.dynamic_slice_in_dim(occ_lam, slab_index * NI, NI, 1).astype(jnp.float32)
    pair_coef = occ_sig.astype(jnp.float32).T[:, None, None, :] * lam_cols.T[None, :, :, None]
    return pair_coef.reshape(nj_all, NI, KL * KS).astype(jnp.bfloat16)


def term_order(shell_pairs, slot):
    one, two = shell_pairs[:, 0], shell_pairs[:, 1]
    count = 2 * one.shape[0]
    target = jnp.concatenate([two, jnp.where(one != two, one, NSH)])
    source = jnp.concatenate([one, two])
    block = jnp.concatenate([slot, slot + one.shape[0]])
    key = target * count + jnp.arange(count, dtype=jnp.int32)
    rank = jnp.sum((key[None, :] < key[:, None]).astype(jnp.int32), axis=1)
    here = (rank[None, :] == jnp.arange(count, dtype=jnp.int32)[:, None]).astype(jnp.int32)
    keep = jnp.sum(jnp.where((target[None, :] == target[:, None]) & (key[None, :] < key[:, None]), 1, 0), axis=1)
    keep = (keep > 0).astype(jnp.int32)
    terms = jnp.stack([source, block, keep])
    terms = jnp.sum(here[None] * terms[:, None, :], axis=2)
    shells = jnp.arange(NSH, dtype=jnp.int32)
    upto = jnp.sum((target[None, :] <= shells[:, None]).astype(jnp.int32), axis=1)
    has = jnp.sum((target[None, :] == shells[:, None]).astype(jnp.int32), axis=1)
    return terms, jnp.stack([jnp.maximum(upto - 1, 0), (has > 0).astype(jnp.int32)])


def fused_kernel(
    terms, last, half, coef, out,
    hbuf, cbuf, carry, sums, left, stage,
    hz_send, hz_recv, h_send, h_recv, c_send, c_recv, o_sem,
):
    z = lax.axis_index("ao")
    me = lax.axis_index("mo")

    def flip(step):
        return me + step * (1 - 2 * lax.rem(me // step, 2))

    sibling = flip(1)
    across_x = flip(2)
    across_y = flip(4)
    across_d = across_x + across_y - me
    barrier = pltpu.get_barrier_semaphore()
    for peer in (sibling, across_x, across_y, across_d):
        pl.semaphore_signal(barrier, inc=1, device_id={"mo": peer}, device_id_type=MESH)
    for d in range(1, 4):
        pl.semaphore_signal(barrier, inc=1, device_id={"ao": lax.rem(z + d, 4)}, device_id_type=MESH)
    pl.semaphore_wait(barrier, 7)

    def send(src, dst, send_sem, recv_sem, device):
        copy = pltpu.make_async_remote_copy(
            src_ref=src, dst_ref=dst, send_sem=send_sem, recv_sem=recv_sem,
            device_id=device, device_id_type=MESH,
        )
        copy.start()
        return copy

    shells_half = NSH // 2
    low, high = pl.ds(0, shells_half), pl.ds(shells_half, shells_half)

    def send_coef(src, slot, part, index, peer):
        return send(src, cbuf.at[slot, part], c_send.at[index], c_recv.at[index], {"mo": peer})

    c_copies = {}
    z_copies = [
        send(half.at[lax.rem(z + d, 4)], hbuf.at[z], hz_send.at[d - 1], hz_recv.at[d - 1], {"ao": lax.rem(z + d, 4)})
        for d in range(1, 4)
    ]
    c_copies["xh"] = send_coef(coef.at[high], 2, high, 0, across_x)
    c_copies["yl"] = send_coef(coef.at[low], 4, low, 1, across_y)
    hbuf[z] = half[z]
    for copy in z_copies:
        copy.wait()

    def send_half(src_slot, dst_slot, index, peer):
        return send(
            hbuf.at[pl.ds(4 * src_slot, 4)], hbuf.at[pl.ds(4 * dst_slot, 4)],
            h_send.at[index], h_recv.at[index], {"mo": peer},
        )

    h_d = send_half(0, 6, 5, across_d)
    h_x = send_half(0, 2, 1, across_x)
    h_y = send_half(0, 4, 3, across_y)
    h_s = send_half(0, 1, 0, sibling)
    c_copies["xl"] = send_coef(coef.at[low], 2, low, 2, across_x)
    c_copies["yh"] = send_coef(coef.at[high], 4, high, 3, across_y)
    c_copies["s"] = send_coef(coef, 1, pl.ds(0, NSH), 4, sibling)
    h_x.wait_recv()
    h_sx = send_half(2, 3, 2, sibling)
    h_y.wait_recv()
    h_sy = send_half(4, 5, 4, sibling)
    h_d.wait_recv()
    h_sd = send_half(6, 7, 6, sibling)
    c_copies["xh"].wait_recv()
    c_copies["dh"] = send_coef(cbuf.at[2, high], 6, high, 5, across_y)
    c_copies["yl"].wait_recv()
    c_copies["dl"] = send_coef(cbuf.at[4, low], 6, low, 6, across_x)
    for copy in (h_s, h_sx, h_sy, h_sd):
        copy.wait()
    for copy in (h_x, h_y, h_d):
        copy.wait_send()

    blocks = 32
    rows = 8

    def turn(block, _):
        values = hbuf[block].astype(jnp.float32).T
        turned = jnp.concatenate([values[r * SH:(r + 1) * SH, :] for r in range(rows)], axis=1)
        hbuf[block + blocks] = turned.astype(jnp.bfloat16)
        return 0

    lax.fori_loop(0, blocks, turn, 0)
    carry[...] = jnp.zeros_like(carry)

    def add_term(t, _):
        added = lax.dot_general(
            coef[terms[0, t]], hbuf[terms[1, t]], (((0,), (0,)), ((), ())), preferred_element_type=jnp.float32
        )
        total = jnp.where(terms[2, t] > 0, carry[...], 0.0) + added
        carry[...] = total
        sums[t] = total.astype(jnp.bfloat16)
        return 0

    lax.fori_loop(0, 2 * blocks, add_term, 0)

    c_copies["xl"].wait_recv()
    c_copies["sx"] = send_coef(cbuf.at[2], 3, pl.ds(0, NSH), 7, sibling)
    c_copies["yh"].wait_recv()
    c_copies["sy"] = send_coef(cbuf.at[4], 5, pl.ds(0, NSH), 8, sibling)

    width = coef.shape[2]

    def place(u, _):
        zero = jnp.zeros((width, rows * SH), jnp.bfloat16)
        first = jnp.where(last[1, 2 * u] > 0, sums[last[0, 2 * u]], zero)
        second = jnp.where(last[1, 2 * u + 1] > 0, sums[last[0, 2 * u + 1]], zero)
        columns = pl.ds(pl.multiple_of(u * 2 * SH, 2 * SH), 2 * SH)
        for r in range(rows):
            both = jnp.concatenate([first[:, r * SH:(r + 1) * SH], second[:, r * SH:(r + 1) * SH]], axis=1)
            left[r * width:(r + 1) * width, columns] = both
        return 0

    lax.fori_loop(0, NSH // 2, place, 0)

    out_copies = [None, None]
    height = 2 * width

    def panel(step, slot):
        buf = step % 2
        if out_copies[buf] is not None:
            out_copies[buf].wait()
        ref = coef if slot == 0 else cbuf.at[slot]

        def tile(m, _):
            part = jnp.dot(
                left[pl.ds(pl.multiple_of(m * height, height), height), :],
                ref[...].reshape(NSH * SH, width),
                preferred_element_type=jnp.float32,
            ).astype(jnp.bfloat16)
            stage[buf, pl.ds(m * 2, 2)] = part.reshape(2, width, width)
            return 0

        lax.fori_loop(0, rows // 2, tile, 0)
        source = me
        for bit in (1, 2, 4):
            if slot & bit:
                source = source + flip(bit) - me
        columns = pl.ds(pl.multiple_of(source * width, width), width)
        copy = pltpu.make_async_copy(stage.at[buf], out.at[:, :, columns], o_sem.at[buf])
        copy.start()
        out_copies[buf] = copy

    panel(0, 0)
    c_copies["s"].wait_recv()
    panel(1, 1)
    panel(2, 2)
    c_copies["dh"].wait_recv()
    c_copies["dl"].wait_recv()
    c_copies["sd"] = send_coef(cbuf.at[6], 7, pl.ds(0, NSH), 9, sibling)
    panel(3, 4)
    c_copies["sx"].wait_recv()
    panel(4, 3)
    c_copies["sy"].wait_recv()
    panel(5, 5)
    panel(6, 6)
    c_copies["sd"].wait_recv()
    panel(7, 7)
    for copy in c_copies.values():
        copy.wait_send()
    for copy in out_copies:
        copy.wait()


def fused_body(pair_ints, shell_pairs, occ_lam, occ_sig, coef_act, slabs):
    width = coef_act.shape[1]
    blocks = shell_pairs.shape[0]
    me = lax.axis_index("mo").astype(jnp.int32)
    number = jnp.arange(blocks, dtype=jnp.int32)
    slot = jnp.bitwise_xor(number % 8, me) * 4 + number // 8
    terms, last = term_order(shell_pairs, slot)
    pair_coef = jnp.stack([pair_coefficients(occ_lam, occ_sig, slabs[k]) for k in range(2)], axis=1)
    rows = 2 * NI
    half = jnp.einsum(
        "mnw,jrw->jmrn", pair_ints.reshape(SH, SH, KL * KS), pair_coef.reshape(4, rows, KL * KS),
        preferred_element_type=jnp.float32,
    ).astype(jnp.bfloat16).reshape(4, SH, rows * SH)
    coef = coef_act.reshape(NSH, SH, width)
    dma = pltpu.SemaphoreType.DMA
    vmem = pl.BlockSpec(memory_space=pltpu.VMEM)
    smem = pl.BlockSpec(memory_space=pltpu.SMEM)
    result = pl.pallas_call(
        fused_kernel,
        out_shape=jax.ShapeDtypeStruct((rows, width, ACT), jnp.bfloat16),
        in_specs=[smem, smem, vmem, vmem],
        out_specs=pl.BlockSpec(memory_space=pl.ANY),
        scratch_shapes=[
            pltpu.VMEM((2 * blocks, SH, rows * SH), jnp.bfloat16),
            pltpu.VMEM((8, NSH, SH, width), jnp.bfloat16),
            pltpu.VMEM((width, rows * SH), jnp.float32),
            pltpu.VMEM((2 * blocks, width, rows * SH), jnp.bfloat16),
            pltpu.VMEM((rows * width, NSH * SH), jnp.bfloat16),
            pltpu.VMEM((2, rows, width, width), jnp.bfloat16),
            dma((3,)), dma((3,)), dma((7,)), dma((7,)), dma((10,)), dma((10,)), dma((2,)),
        ],
        compiler_params=pltpu.CompilerParams(
            collective_id=0, has_side_effects=True, vmem_limit_bytes=56 * 2 ** 20
        ),
        cost_estimate=pl.CostEstimate(
            flops=2 * rows * width * ACT * ACT, bytes_accessed=12 * 2 ** 20, transcendentals=0
        ),
    )(terms, last, half, coef)
    return result.reshape(2, 1, NI, width, ACT)


def ket_transform(pair_ints, occ_lam, occ_sig, slab_index):
    blocks_here = pair_ints.shape[0]
    nj_all = occ_sig.shape[1]
    pair_coef = pair_coefficients(occ_lam, occ_sig, slab_index).reshape(nj_all * NI, KL * KS)
    half_ints = jnp.einsum("bqw,xw->bxq", pair_ints, pair_coef, preferred_element_type=jnp.float32)
    return half_ints.astype(jnp.bfloat16).reshape(blocks_here, nj_all, NI, SH * SH)


def remap_pairs(stacked):
    owned = lax.all_to_all(stacked, "ao", split_axis=2, concat_axis=1, tiled=True)
    return lax.all_gather(owned, "mo", axis=1, tiled=True)


def general_body(pair_ints, shell_pairs, occ_lam, occ_sig, coef_act, slabs):
    ao_count = lax.axis_size("ao")
    mo_count = lax.axis_size("mo")
    blocks_here = pair_ints.shape[0]
    panel_width = coef_act.shape[1]
    ao_width = coef_act.shape[0]
    ordered_pairs = (
        shell_pairs.reshape(ao_count, mo_count, blocks_here, 2).transpose(1, 0, 2, 3).reshape(-1, 2)
    )
    halves = [ket_transform(pair_ints, occ_lam, occ_sig, slabs[k]) for k in range(2)]
    gathered_slabs = [remap_pairs(single[None])[0] for single in halves]
    coef_shells = coef_act.reshape(NSH, SH, panel_width)
    coef_all = lax.all_gather(coef_act, "mo", axis=1, tiled=True)

    def bra_transform(gathered):
        block_count = gathered.shape[0]
        pair_rows = gathered.shape[1] * gathered.shape[2]
        blocks = gathered.reshape(block_count, pair_rows, SH, SH)

        def accumulate(running, item):
            values, pair = item
            term_one = jnp.einsum(
                "rmn,ma->ran", values, coef_shells[pair[0]], preferred_element_type=jnp.float32
            )
            term_two = jnp.einsum(
                "rmn,na->ram", values, coef_shells[pair[1]], preferred_element_type=jnp.float32
            ) * (pair[0] != pair[1]).astype(jnp.float32)
            running = running.at[pair[1]].add(term_one)
            return running.at[pair[0]].add(term_two), None

        start_terms = jnp.zeros((NSH, pair_rows, panel_width, SH), jnp.float32)
        left_terms = lax.scan(accumulate, start_terms, (blocks, ordered_pairs))[0]
        left_rounded = left_terms.astype(jnp.bfloat16).transpose(1, 2, 0, 3)
        product = jnp.dot(
            left_rounded.reshape(pair_rows * panel_width, ao_width), coef_all, preferred_element_type=jnp.float32
        )
        return product.astype(jnp.bfloat16).reshape(gathered.shape[1], NI, panel_width, ACT)

    return jnp.stack([bra_transform(gathered) for gathered in gathered_slabs])


def solution(mesh):
    fits = mesh.shape["ao"] == 4 and mesh.shape["mo"] == 8
    return jax.shard_map(
        fused_body if fits else general_body,
        mesh=mesh,
        in_specs=(P(("ao", "mo"), None, None), P(), P(), P(), P(None, "mo"), P()),
        out_specs=P(None, "ao", None, "mo", None),
        check_vma=False,
    )
```

```python
import functools

import jax
import jax.numpy as jnp
from jax import lax
from jax.experimental import pallas as pl
from jax.experimental.pallas import tpu as pltpu
from jax.sharding import PartitionSpec as P

SH = 64
NSH = 32
ACT = 2048
KL = 16
KS = 16
NI = 4
MESH = pl.DeviceIdType.MESH
FIRST = (0, 1, 2, 4)
SECOND = (3, 5, 6, 7)


def pair_coefficients(occ_lam, occ_sig, slab_index):
    nj_all = occ_sig.shape[1]
    lam_cols = lax.dynamic_slice_in_dim(occ_lam, slab_index * NI, NI, 1).astype(jnp.float32)
    pair_coef = occ_sig.astype(jnp.float32).T[:, None, None, :] * lam_cols.T[None, :, :, None]
    return pair_coef.reshape(nj_all, NI, KL * KS).astype(jnp.bfloat16)


def prepare_kernel(slabs, me, pairs, occ_lam, occ_sig, terms, last, pair_coef):
    blocks = pairs.shape[0]
    count = 2 * blocks
    numbers = pairs[...]
    one, two = numbers[:, 0:1], numbers[:, 1:2]
    block = lax.broadcasted_iota(jnp.int32, (blocks, 1), 0)
    slot = jnp.bitwise_xor(lax.rem(block, 8), jnp.full((blocks, 1), me[0], jnp.int32)) * 4 + block // 8
    real = jnp.float32
    target = jnp.concatenate([two, jnp.where(one != two, one, NSH)], axis=0).astype(real)
    source = jnp.concatenate([one, two], axis=0).astype(real)
    place = jnp.concatenate([slot, slot + blocks], axis=0).astype(real)
    down = lax.broadcasted_iota(jnp.int32, (count, count), 0)
    along = lax.broadcasted_iota(jnp.int32, (count, count), 1)
    target_down = jnp.broadcast_to(target, (count, count))
    target_along = jnp.broadcast_to(
        jnp.sum(jnp.where(down == along, target_down, 0.0), axis=0, keepdims=True), (count, count)
    )
    earlier = (target_along < target_down) | ((target_along == target_down) & (along < down))
    rank = jnp.sum(jnp.where(earlier, 1.0, 0.0), axis=1, keepdims=True)
    same = jnp.sum(jnp.where((target_along == target_down) & (along < down), 1.0, 0.0), axis=1, keepdims=True)
    keep = jnp.where(same > 0.0, 1.0, 0.0)
    here = rank == along.astype(real)
    for row, column in enumerate((source, place, keep)):
        terms[row:row + 1, :] = jnp.sum(jnp.where(here, column, 0.0), axis=0, keepdims=True).astype(jnp.int32)
    shells = lax.broadcasted_iota(jnp.int32, (count, NSH), 1).astype(real)
    upto = jnp.sum(jnp.where(target <= shells, 1.0, 0.0), axis=0, keepdims=True)
    has = jnp.sum(jnp.where(target == shells, 1.0, 0.0), axis=0, keepdims=True)
    last[0:1, :] = jnp.maximum(upto - 1.0, 0.0).astype(jnp.int32)
    last[1:2, :] = jnp.minimum(has, 1.0).astype(jnp.int32)

    rows, occupied = pair_coef.shape[0], occ_lam.shape[1]
    nj_all = occ_sig.shape[1]
    half = jnp.bfloat16

    def pick(chosen, values, spread):
        some = lax.dot_general(
            jnp.where(chosen, 1.0, 0.0).astype(half), values, (((1,), (1,)), ((), ())), preferred_element_type=real
        )
        return jnp.dot(some.astype(half), jnp.where(spread, 1.0, 0.0).astype(half), preferred_element_type=real)

    row = lax.broadcasted_iota(jnp.int32, (rows, occupied), 0)
    column = lax.broadcasted_iota(jnp.int32, (rows, occupied), 1)
    wanted = jnp.where(lax.rem(row // NI, 2) == 0, slabs[0], slabs[1]) * NI + lax.rem(row, NI)
    row_j = lax.broadcasted_iota(jnp.int32, (rows, nj_all), 0)
    column_j = lax.broadcasted_iota(jnp.int32, (rows, nj_all), 1)
    pair = lax.broadcasted_iota(jnp.int32, (KL, KL * KS), 1)
    single = lax.broadcasted_iota(jnp.int32, (KL, KL * KS), 0)
    lam = pick(column == wanted, occ_lam[...], pair // KS == single)
    sig = pick(column_j == row_j // (2 * NI), occ_sig[...], lax.rem(pair, KS) == single)
    pair_coef[...] = (lam * sig).astype(half)


def rest_kernel(me, left, coefs, done, out, lbuf, cbuf, stage, l_sem, c_sem, d_sem, o_sem):
    width = cbuf.shape[2]
    rows = done.shape[1]
    height = 2 * width

    def columns(slot):
        return pl.ds(pl.multiple_of(jnp.bitwise_xor(me[0], slot) * width, width), width)

    loads = [pltpu.make_async_copy(coefs.at[n], cbuf.at[n], c_sem.at[n]) for n in range(4)]
    lefts = [
        pltpu.make_async_copy(left.at[pl.ds(m * height, height)], lbuf.at[m], l_sem.at[m]) for m in range(rows // 2)
    ]
    loads[0].start()
    lefts[0].start()
    for copy in loads[1:] + lefts[1:]:
        copy.start()
    moves = [
        pltpu.make_async_copy(done.at[n], out.at[:, :, columns(slot)], d_sem.at[n])
        for n, slot in enumerate(FIRST)
    ]
    for copy in moves:
        copy.start()
    stores = []
    for m in range(rows // 2):
        lefts[m].wait()
        for n, slot in enumerate(SECOND):
            if m == 0:
                loads[n].wait()
            part = jnp.dot(lbuf[m], cbuf[n], preferred_element_type=jnp.float32).astype(jnp.bfloat16)
            stage[m, n] = part.reshape(2, width, width)
            copy = pltpu.make_async_copy(
                stage.at[m, n], out.at[pl.ds(2 * m, 2), :, columns(slot)], o_sem.at[m, n]
            )
            copy.start()
            stores.append(copy)
    for copy in moves + stores:
        copy.wait()


def fused_kernel(
    terms, last, half, coef, left_out, coefs_out, out,
    hbuf, cbuf, carry, sums, left, stage,
    hz_send, hz_recv, h_send, h_recv, c_send, c_recv, o_sem, l_sem, k_sem,
):
    z = lax.axis_index("ao")
    me = lax.axis_index("mo")

    def flip(step):
        return me + step * (1 - 2 * lax.rem(me // step, 2))

    sibling = flip(1)
    across_x = flip(2)
    across_y = flip(4)
    across_d = across_x + across_y - me
    barrier = pltpu.get_barrier_semaphore()
    for peer in (sibling, across_x, across_y, across_d):
        pl.semaphore_signal(barrier, inc=1, device_id={"mo": peer}, device_id_type=MESH)
    for d in range(1, 4):
        pl.semaphore_signal(barrier, inc=1, device_id={"ao": lax.rem(z + d, 4)}, device_id_type=MESH)
    pl.semaphore_wait(barrier, 7)

    def send(src, dst, send_sem, recv_sem, device):
        copy = pltpu.make_async_remote_copy(
            src_ref=src, dst_ref=dst, send_sem=send_sem, recv_sem=recv_sem,
            device_id=device, device_id_type=MESH,
        )
        copy.start()
        return copy

    blocks = 32
    rows = 8
    quarter = NSH // 4
    low, high = pl.ds(0, 2 * quarter), pl.ds(2 * quarter, 2 * quarter)
    parts = [pl.ds(n * quarter, quarter) for n in range(4)]

    def send_coef(src, slot, part, index, peer):
        return send(src, cbuf.at[slot, part], c_send.at[index], c_recv.at[index], {"mo": peer})

    def turn(block, _):
        values = hbuf[block].astype(jnp.float32).T
        turned = jnp.concatenate([values[r * SH:(r + 1) * SH, :] for r in range(rows)], axis=1)
        hbuf[block + blocks] = turned.astype(jnp.bfloat16)
        return 0

    def turn_slot(slot):
        lax.fori_loop(4 * slot, 4 * slot + 4, turn, 0)

    c_copies = {}
    z_copies = [
        send(half.at[lax.rem(z + d, 4)], hbuf.at[z], hz_send.at[d - 1], hz_recv.at[d - 1], {"ao": lax.rem(z + d, 4)})
        for d in range(1, 4)
    ]
    c_copies["x2"] = send_coef(coef.at[parts[2]], 2, parts[2], 0, across_x)
    c_copies["y0"] = send_coef(coef.at[parts[0]], 4, parts[0], 1, across_y)
    hbuf[z] = half[z]
    for copy in z_copies:
        copy.wait()

    def send_half(src_slot, dst_slot, index, peer):
        return send(
            hbuf.at[pl.ds(4 * src_slot, 4)], hbuf.at[pl.ds(4 * dst_slot, 4)],
            h_send.at[index], h_recv.at[index], {"mo": peer},
        )

    h_d = send_half(0, 6, 5, across_d)
    h_x = send_half(0, 2, 1, across_x)
    h_y = send_half(0, 4, 3, across_y)
    h_s = send_half(0, 1, 0, sibling)
    c_copies["s"] = send_coef(coef, 1, pl.ds(0, NSH), 4, sibling)
    turn_slot(0)
    h_s.wait_recv()
    turn_slot(1)
    h_x.wait_recv()
    h_sx = send_half(2, 3, 2, sibling)
    h_y.wait_recv()
    h_sy = send_half(4, 5, 4, sibling)
    c_copies["x3"] = send_coef(coef.at[parts[3]], 2, parts[3], 10, across_x)
    c_copies["y1"] = send_coef(coef.at[parts[1]], 4, parts[1], 11, across_y)
    c_copies["xl"] = send_coef(coef.at[low], 2, low, 2, across_x)
    c_copies["yh"] = send_coef(coef.at[high], 4, high, 3, across_y)
    turn_slot(2)
    turn_slot(4)
    h_d.wait_recv()
    h_sd = send_half(6, 7, 6, sibling)
    h_sx.wait_recv()
    turn_slot(3)
    h_sy.wait_recv()
    turn_slot(5)
    turn_slot(6)
    h_sd.wait_recv()
    turn_slot(7)
    for copy in (h_s, h_x, h_y, h_d, h_sx, h_sy, h_sd):
        copy.wait_send()
    carry[...] = jnp.zeros_like(carry)

    def add_term(t, _):
        added = lax.dot_general(
            coef[terms[0, t]], hbuf[terms[1, t]], (((0,), (0,)), ((), ())), preferred_element_type=jnp.float32
        )
        total = jnp.where(terms[2, t] > 0, carry[...], 0.0) + added
        carry[...] = total
        sums[t] = total.astype(jnp.bfloat16)
        return 0

    lax.fori_loop(0, blocks, add_term, 0)
    c_copies["x2"].wait_recv()
    c_copies["x3"].wait_recv()
    c_copies["dh"] = send_coef(cbuf.at[2, high], 6, high, 5, across_y)
    c_copies["y0"].wait_recv()
    c_copies["y1"].wait_recv()
    c_copies["dl"] = send_coef(cbuf.at[4, low], 6, low, 6, across_x)
    lax.fori_loop(blocks, 2 * blocks, add_term, 0)

    c_copies["xl"].wait_recv()
    c_copies["sx"] = send_coef(cbuf.at[2], 3, pl.ds(0, NSH), 7, sibling)
    c_copies["yh"].wait_recv()
    c_copies["sy"] = send_coef(cbuf.at[4], 5, pl.ds(0, NSH), 8, sibling)

    width = coef.shape[2]

    def place(u, _):
        zero = jnp.zeros((width, rows * SH), jnp.bfloat16)
        first = jnp.where(last[1, 2 * u] > 0, sums[last[0, 2 * u]], zero)
        second = jnp.where(last[1, 2 * u + 1] > 0, sums[last[0, 2 * u + 1]], zero)
        columns = pl.ds(pl.multiple_of(u * 2 * SH, 2 * SH), 2 * SH)
        for r in range(rows):
            both = jnp.concatenate([first[:, r * SH:(r + 1) * SH], second[:, r * SH:(r + 1) * SH]], axis=1)
            left[r * width:(r + 1) * width, columns] = both
        return 0

    lax.fori_loop(0, NSH // 2, place, 0)

    left_copy = pltpu.make_async_copy(left, left_out, l_sem)
    left_copy.start()
    out_copies = [None, None]
    height = 2 * width

    def panel(step, slot):
        buf = step % 2
        if out_copies[buf] is not None:
            out_copies[buf].wait()
        ref = coef if slot == 0 else cbuf.at[slot]

        def tile(m, _):
            part = jnp.dot(
                left[pl.ds(pl.multiple_of(m * height, height), height), :],
                ref[...].reshape(NSH * SH, width),
                preferred_element_type=jnp.float32,
            ).astype(jnp.bfloat16)
            stage[buf, pl.ds(m * 2, 2)] = part.reshape(2, width, width)
            return 0

        lax.fori_loop(0, rows // 2, tile, 0)
        copy = pltpu.make_async_copy(stage.at[buf], out.at[step], o_sem.at[buf])
        copy.start()
        out_copies[buf] = copy

    panel(0, FIRST[0])
    c_copies["s"].wait_recv()
    panel(1, FIRST[1])
    c_copies["dh"].wait_recv()
    c_copies["dl"].wait_recv()
    c_copies["sd"] = send_coef(cbuf.at[6], 7, pl.ds(0, NSH), 9, sibling)
    panel(2, FIRST[2])
    panel(3, FIRST[3])
    for name in ("sx", "sy", "sd"):
        c_copies[name].wait_recv()
    coef_copies = [pltpu.make_async_copy(cbuf.at[slot], coefs_out.at[n], k_sem.at[n]) for n, slot in enumerate(SECOND)]
    for copy in coef_copies:
        copy.start()
    for copy in c_copies.values():
        copy.wait_send()
    for copy in coef_copies + out_copies + [left_copy]:
        copy.wait()


def fused_body(pair_ints, shell_pairs, occ_lam, occ_sig, coef_act, slabs):
    width = coef_act.shape[1]
    blocks = shell_pairs.shape[0]
    me = lax.axis_index("mo").astype(jnp.int32)
    here = me.reshape(1)
    rows = 2 * NI
    vmem = pl.BlockSpec(memory_space=pltpu.VMEM)
    smem = pl.BlockSpec(memory_space=pltpu.SMEM)
    hbm = pl.BlockSpec(memory_space=pl.ANY)
    terms, last, pair_coef = pl.pallas_call(
        prepare_kernel,
        out_shape=(
            jax.ShapeDtypeStruct((3, 2 * blocks), jnp.int32),
            jax.ShapeDtypeStruct((2, NSH), jnp.int32),
            jax.ShapeDtypeStruct((4 * rows, KL * KS), jnp.bfloat16),
        ),
        in_specs=[smem, smem, vmem, vmem, vmem],
        out_specs=(vmem, vmem, vmem),
    )(slabs, here, shell_pairs, occ_lam, occ_sig)
    half = jnp.einsum(
        "mnw,jrw->jmrn", pair_ints.reshape(SH, SH, KL * KS), pair_coef.reshape(4, rows, KL * KS),
        preferred_element_type=jnp.float32,
    ).astype(jnp.bfloat16).reshape(4, SH, rows * SH)
    coef = coef_act.reshape(NSH, SH, width)
    dma = pltpu.SemaphoreType.DMA
    left, coefs, done = pl.pallas_call(
        fused_kernel,
        out_shape=(
            jax.ShapeDtypeStruct((rows * width, NSH * SH), jnp.bfloat16),
            jax.ShapeDtypeStruct((4, NSH, SH, width), jnp.bfloat16),
            jax.ShapeDtypeStruct((4, rows, width, width), jnp.bfloat16),
        ),
        in_specs=[smem, smem, vmem, vmem],
        out_specs=(hbm, hbm, hbm),
        scratch_shapes=[
            pltpu.VMEM((2 * blocks, SH, rows * SH), jnp.bfloat16),
            pltpu.VMEM((8, NSH, SH, width), jnp.bfloat16),
            pltpu.VMEM((width, rows * SH), jnp.float32),
            pltpu.VMEM((2 * blocks, width, rows * SH), jnp.bfloat16),
            pltpu.VMEM((rows * width, NSH * SH), jnp.bfloat16),
            pltpu.VMEM((2, rows, width, width), jnp.bfloat16),
            dma((3,)), dma((3,)), dma((7,)), dma((7,)), dma((12,)), dma((12,)), dma((2,)),
            dma, dma((4,)),
        ],
        compiler_params=pltpu.CompilerParams(
            collective_id=0, has_side_effects=True, vmem_limit_bytes=56 * 2 ** 20
        ),
        cost_estimate=pl.CostEstimate(
            flops=rows * width * ACT * ACT, bytes_accessed=12 * 2 ** 20, transcendentals=0
        ),
    )(terms, last, half, coef)
    result = pl.pallas_call(
        rest_kernel,
        out_shape=jax.ShapeDtypeStruct((rows, width, ACT), jnp.bfloat16),
        in_specs=[smem, hbm, hbm, hbm],
        out_specs=hbm,
        scratch_shapes=[
            pltpu.VMEM((rows // 2, 2 * width, NSH * SH), jnp.bfloat16),
            pltpu.VMEM((4, NSH * SH, width), jnp.bfloat16),
            pltpu.VMEM((rows // 2, 4, 2, width, width), jnp.bfloat16),
            dma((rows // 2,)), dma((4,)), dma((4,)), dma((rows // 2, 4)),
        ],
        compiler_params=pltpu.CompilerParams(vmem_limit_bytes=56 * 2 ** 20),
        cost_estimate=pl.CostEstimate(
            flops=rows * width * ACT * ACT, bytes_accessed=24 * 2 ** 20, transcendentals=0
        ),
    )(here, left, coefs.reshape(4, NSH * SH, width), done)
    return result.reshape(2, 1, NI, width, ACT)


def ket_transform(pair_ints, occ_lam, occ_sig, slab_index):
    blocks_here = pair_ints.shape[0]
    nj_all = occ_sig.shape[1]
    pair_coef = pair_coefficients(occ_lam, occ_sig, slab_index).reshape(nj_all * NI, KL * KS)
    half_ints = jnp.einsum("bqw,xw->bxq", pair_ints, pair_coef, preferred_element_type=jnp.float32)
    return half_ints.astype(jnp.bfloat16).reshape(blocks_here, nj_all, NI, SH * SH)


def remap_pairs(stacked):
    owned = lax.all_to_all(stacked, "ao", split_axis=2, concat_axis=1, tiled=True)
    return lax.all_gather(owned, "mo", axis=1, tiled=True)


def general_body(pair_ints, shell_pairs, occ_lam, occ_sig, coef_act, slabs):
    ao_count = lax.axis_size("ao")
    mo_count = lax.axis_size("mo")
    blocks_here = pair_ints.shape[0]
    panel_width = coef_act.shape[1]
    ao_width = coef_act.shape[0]
    ordered_pairs = (
        shell_pairs.reshape(ao_count, mo_count, blocks_here, 2).transpose(1, 0, 2, 3).reshape(-1, 2)
    )
    halves = [ket_transform(pair_ints, occ_lam, occ_sig, slabs[k]) for k in range(2)]
    gathered_slabs = [remap_pairs(single[None])[0] for single in halves]
    coef_shells = coef_act.reshape(NSH, SH, panel_width)
    coef_all = lax.all_gather(coef_act, "mo", axis=1, tiled=True)

    def bra_transform(gathered):
        block_count = gathered.shape[0]
        pair_rows = gathered.shape[1] * gathered.shape[2]
        blocks = gathered.reshape(block_count, pair_rows, SH, SH)

        def accumulate(running, item):
            values, pair = item
            term_one = jnp.einsum(
                "rmn,ma->ran", values, coef_shells[pair[0]], preferred_element_type=jnp.float32
            )
            term_two = jnp.einsum(
                "rmn,na->ram", values, coef_shells[pair[1]], preferred_element_type=jnp.float32
            ) * (pair[0] != pair[1]).astype(jnp.float32)
            running = running.at[pair[1]].add(term_one)
            return running.at[pair[0]].add(term_two), None

        start_terms = jnp.zeros((NSH, pair_rows, panel_width, SH), jnp.float32)
        left_terms = lax.scan(accumulate, start_terms, (blocks, ordered_pairs))[0]
        left_rounded = left_terms.astype(jnp.bfloat16).transpose(1, 2, 0, 3)
        product = jnp.dot(
            left_rounded.reshape(pair_rows * panel_width, ao_width), coef_all, preferred_element_type=jnp.float32
        )
        return product.astype(jnp.bfloat16).reshape(gathered.shape[1], NI, panel_width, ACT)

    return jnp.stack([bra_transform(gathered) for gathered in gathered_slabs])


def solution(mesh):
    fits = mesh.shape["ao"] == 4 and mesh.shape["mo"] == 8
    return jax.shard_map(
        fused_body if fits else general_body,
        mesh=mesh,
        in_specs=(P(("ao", "mo"), None, None), P(), P(), P(), P(None, "mo"), P()),
        out_specs=P(None, "ao", None, "mo", None),
        check_vma=False,
    )
```

```python
import functools

import jax
import jax.numpy as jnp
from jax import lax
from jax.experimental import pallas as pl
from jax.experimental.pallas import tpu as pltpu
from jax.sharding import PartitionSpec as P

SH = 64
NSH = 32
ACT = 2048
KL = 16
KS = 16
NI = 4
MESH = pl.DeviceIdType.MESH
FIRST = (0, 1, 2, 4)
SECOND = (3, 5, 6, 7)


def pair_coefficients(occ_lam, occ_sig, slab_index):
    nj_all = occ_sig.shape[1]
    lam_cols = lax.dynamic_slice_in_dim(occ_lam, slab_index * NI, NI, 1).astype(jnp.float32)
    pair_coef = occ_sig.astype(jnp.float32).T[:, None, None, :] * lam_cols.T[None, :, :, None]
    return pair_coef.reshape(nj_all, NI, KL * KS).astype(jnp.bfloat16)


def prepare_kernel(slabs, me, pairs, occ_lam, occ_sig, terms, last, pair_coef):
    blocks = pairs.shape[1]
    count = 2 * blocks
    numbers = pairs[...].astype(jnp.float32)
    diagonal = lax.broadcasted_iota(jnp.int32, (blocks, blocks), 0) == lax.broadcasted_iota(
        jnp.int32, (blocks, blocks), 1
    )
    one, two = (
        jnp.sum(jnp.where(diagonal, numbers[n:n + 1, :], 0.0), axis=1, keepdims=True).astype(jnp.int32)
        for n in range(2)
    )
    block = lax.broadcasted_iota(jnp.int32, (blocks, 1), 0)
    slot = jnp.bitwise_xor(lax.rem(block, 8), jnp.full((blocks, 1), me[0], jnp.int32)) * 4 + block // 8
    real = jnp.float32
    target = jnp.concatenate([two, jnp.where(one != two, one, NSH)], axis=0).astype(real)
    source = jnp.concatenate([one, two], axis=0).astype(real)
    place = jnp.concatenate([slot, slot + blocks], axis=0).astype(real)
    down = lax.broadcasted_iota(jnp.int32, (count, count), 0)
    along = lax.broadcasted_iota(jnp.int32, (count, count), 1)
    target_down = jnp.broadcast_to(target, (count, count))
    target_along = jnp.broadcast_to(
        jnp.sum(jnp.where(down == along, target_down, 0.0), axis=0, keepdims=True), (count, count)
    )
    earlier = (target_along < target_down) | ((target_along == target_down) & (along < down))
    rank = jnp.sum(jnp.where(earlier, 1.0, 0.0), axis=1, keepdims=True)
    same = jnp.sum(jnp.where((target_along == target_down) & (along < down), 1.0, 0.0), axis=1, keepdims=True)
    keep = jnp.where(same > 0.0, 1.0, 0.0)
    here = rank == along.astype(real)
    for row, column in enumerate((source, place, keep)):
        terms[row:row + 1, :] = jnp.sum(jnp.where(here, column, 0.0), axis=0, keepdims=True).astype(jnp.int32)
    shells = lax.broadcasted_iota(jnp.int32, (count, NSH), 1).astype(real)
    upto = jnp.sum(jnp.where(target <= shells, 1.0, 0.0), axis=0, keepdims=True)
    has = jnp.sum(jnp.where(target == shells, 1.0, 0.0), axis=0, keepdims=True)
    last[0:1, :] = jnp.maximum(upto - 1.0, 0.0).astype(jnp.int32)
    last[1:2, :] = jnp.minimum(has, 1.0).astype(jnp.int32)

    rows, occupied = pair_coef.shape[0], occ_lam.shape[1]
    nj_all = occ_sig.shape[0]
    half = jnp.bfloat16

    def pick(chosen, values, spread, contract):
        some = lax.dot_general(
            jnp.where(chosen, 1.0, 0.0).astype(half), values, (((1,), (contract,)), ((), ())),
            preferred_element_type=real,
        )
        return jnp.dot(some.astype(half), jnp.where(spread, 1.0, 0.0).astype(half), preferred_element_type=real)

    row = lax.broadcasted_iota(jnp.int32, (rows, occupied), 0)
    column = lax.broadcasted_iota(jnp.int32, (rows, occupied), 1)
    wanted = jnp.where(lax.rem(row // NI, 2) == 0, slabs[0], slabs[1]) * NI + lax.rem(row, NI)
    row_j = lax.broadcasted_iota(jnp.int32, (rows, nj_all), 0)
    column_j = lax.broadcasted_iota(jnp.int32, (rows, nj_all), 1)
    pair = lax.broadcasted_iota(jnp.int32, (KL, KL * KS), 1)
    single = lax.broadcasted_iota(jnp.int32, (KL, KL * KS), 0)
    lam = pick(column == wanted, occ_lam[...], pair // KS == single, 1)
    sig = pick(column_j == row_j // (2 * NI), occ_sig[...], lax.rem(pair, KS) == single, 0)
    pair_coef[...] = (lam * sig).astype(half)


def rest_kernel(me, left, coefs, done, out, lbuf, cbuf, dbuf, stage, l_sem, c_sem, d_sem, m_sem, o_sem):
    width = cbuf.shape[2]
    rows = done.shape[1]
    height = 2 * width

    def columns(slot):
        return pl.ds(pl.multiple_of(jnp.bitwise_xor(me[0], slot) * width, width), width)

    loads = [pltpu.make_async_copy(coefs.at[n], cbuf.at[n], c_sem.at[n]) for n in range(4)]
    lefts = [
        pltpu.make_async_copy(left.at[pl.ds(m * height, height)], lbuf.at[m], l_sem.at[m]) for m in range(rows // 2)
    ]
    loads[0].start()
    lefts[0].start()
    for copy in loads[1:] + lefts[1:]:
        copy.start()
    fetches = [pltpu.make_async_copy(done.at[n], dbuf.at[n], d_sem.at[n]) for n in range(4)]
    moves = [
        pltpu.make_async_copy(dbuf.at[n], out.at[:, :, columns(slot)], m_sem.at[n]) for n, slot in enumerate(FIRST)
    ]
    for copy in fetches:
        copy.start()
    stores = []
    for m in range(rows // 2):
        lefts[m].wait()
        for n, slot in enumerate(SECOND):
            if m == 0:
                loads[n].wait()
            part = jnp.dot(lbuf[m], cbuf[n], preferred_element_type=jnp.float32).astype(jnp.bfloat16)
            stage[m, n] = part.reshape(2, width, width)
            copy = pltpu.make_async_copy(
                stage.at[m, n], out.at[pl.ds(2 * m, 2), :, columns(slot)], o_sem.at[m, n]
            )
            copy.start()
            stores.append(copy)
        if m < 2:
            for n in (2 * m, 2 * m + 1):
                fetches[n].wait()
                moves[n].start()
    for copy in moves + stores:
        copy.wait()


def fused_kernel(
    terms, last, half, coef, left_out, coefs_out, out,
    hbuf, cbuf, coef_t, carry, sums, left, stage,
    hz_send, hz_recv, h_send, h_recv, c_send, c_recv, o_sem, l_sem, k_sem,
):
    z = lax.axis_index("ao")
    me = lax.axis_index("mo")

    def flip(step):
        return me + step * (1 - 2 * lax.rem(me // step, 2))

    sibling = flip(1)
    across_x = flip(2)
    across_y = flip(4)
    across_d = across_x + across_y - me
    barrier = pltpu.get_barrier_semaphore()
    for peer in (sibling, across_x, across_y, across_d):
        pl.semaphore_signal(barrier, inc=1, device_id={"mo": peer}, device_id_type=MESH)
    for d in range(1, 4):
        pl.semaphore_signal(barrier, inc=1, device_id={"ao": lax.rem(z + d, 4)}, device_id_type=MESH)
    pl.semaphore_wait(barrier, 7)

    def send(src, dst, send_sem, recv_sem, device):
        copy = pltpu.make_async_remote_copy(
            src_ref=src, dst_ref=dst, send_sem=send_sem, recv_sem=recv_sem,
            device_id=device, device_id_type=MESH,
        )
        copy.start()
        return copy

    blocks = 32
    rows = 8
    quarter = NSH // 4
    low, high = pl.ds(0, 2 * quarter), pl.ds(2 * quarter, 2 * quarter)
    parts = [pl.ds(n * quarter, quarter) for n in range(4)]

    def send_coef(src, slot, part, index, peer):
        return send(src, cbuf.at[slot, part], c_send.at[index], c_recv.at[index], {"mo": peer})

    def turn(block, _):
        values = hbuf[block].astype(jnp.float32).T
        turned = jnp.concatenate([values[r * SH:(r + 1) * SH, :] for r in range(rows)], axis=1)
        hbuf[block + blocks] = turned.astype(jnp.bfloat16)
        return 0

    def turn_slot(slot):
        lax.fori_loop(4 * slot, 4 * slot + 4, turn, 0)

    c_copies = {}
    z_copies = [
        send(half.at[lax.rem(z + d, 4)], hbuf.at[z], hz_send.at[d - 1], hz_recv.at[d - 1], {"ao": lax.rem(z + d, 4)})
        for d in range(1, 4)
    ]
    c_copies["x2"] = send_coef(coef.at[parts[2]], 2, parts[2], 0, across_x)
    c_copies["y0"] = send_coef(coef.at[parts[0]], 4, parts[0], 1, across_y)
    hbuf[z] = half[z]

    def turn_coef(shell, _):
        coef_t[shell] = coef[shell].astype(jnp.float32).T.astype(jnp.bfloat16)
        return 0

    lax.fori_loop(0, NSH // 2, turn_coef, 0)
    for copy in z_copies:
        copy.wait()

    def send_half(src_slot, dst_slot, index, peer):
        return send(
            hbuf.at[pl.ds(4 * src_slot, 4)], hbuf.at[pl.ds(4 * dst_slot, 4)],
            h_send.at[index], h_recv.at[index], {"mo": peer},
        )

    h_d = send_half(0, 6, 5, across_d)
    h_x = send_half(0, 2, 1, across_x)
    h_y = send_half(0, 4, 3, across_y)
    h_s = send_half(0, 1, 0, sibling)
    c_copies["s"] = send_coef(coef, 1, pl.ds(0, NSH), 4, sibling)
    lax.fori_loop(NSH // 2, NSH, turn_coef, 0)
    turn_slot(0)
    h_s.wait_recv()
    turn_slot(1)
    h_x.wait_recv()
    h_sx = send_half(2, 3, 2, sibling)
    h_y.wait_recv()
    h_sy = send_half(4, 5, 4, sibling)
    c_copies["x3"] = send_coef(coef.at[parts[3]], 2, parts[3], 10, across_x)
    c_copies["y1"] = send_coef(coef.at[parts[1]], 4, parts[1], 11, across_y)
    c_copies["xl"] = send_coef(coef.at[low], 2, low, 2, across_x)
    c_copies["yh"] = send_coef(coef.at[high], 4, high, 3, across_y)
    turn_slot(2)
    turn_slot(4)
    h_d.wait_recv()
    h_sd = send_half(6, 7, 6, sibling)
    h_sx.wait_recv()
    turn_slot(3)
    h_sy.wait_recv()
    turn_slot(5)
    turn_slot(6)
    h_sd.wait_recv()
    turn_slot(7)
    for copy in (h_s, h_x, h_y, h_d, h_sx, h_sy, h_sd):
        copy.wait_send()
    carry[...] = jnp.zeros_like(carry)

    def add_term(t, _):
        added = jnp.dot(coef_t[terms[0, t]], hbuf[terms[1, t]], preferred_element_type=jnp.float32)
        total = jnp.where(terms[2, t] > 0, carry[...], 0.0) + added
        carry[...] = total
        sums[t] = total.astype(jnp.bfloat16)
        return 0

    lax.fori_loop(0, blocks, add_term, 0)
    c_copies["x2"].wait_recv()
    c_copies["x3"].wait_recv()
    c_copies["dh"] = send_coef(cbuf.at[2, high], 6, high, 5, across_y)
    c_copies["y0"].wait_recv()
    c_copies["y1"].wait_recv()
    c_copies["dl"] = send_coef(cbuf.at[4, low], 6, low, 6, across_x)
    lax.fori_loop(blocks, 2 * blocks, add_term, 0)

    c_copies["xl"].wait_recv()
    c_copies["sx"] = send_coef(cbuf.at[2], 3, pl.ds(0, NSH), 7, sibling)
    c_copies["yh"].wait_recv()
    c_copies["sy"] = send_coef(cbuf.at[4], 5, pl.ds(0, NSH), 8, sibling)

    width = coef.shape[2]

    def place(u, _):
        zero = jnp.zeros((width, rows * SH), jnp.bfloat16)
        first = jnp.where(last[1, 2 * u] > 0, sums[last[0, 2 * u]], zero)
        second = jnp.where(last[1, 2 * u + 1] > 0, sums[last[0, 2 * u + 1]], zero)
        columns = pl.ds(pl.multiple_of(u * 2 * SH, 2 * SH), 2 * SH)
        for r in range(rows):
            both = jnp.concatenate([first[:, r * SH:(r + 1) * SH], second[:, r * SH:(r + 1) * SH]], axis=1)
            left[r * width:(r + 1) * width, columns] = both
        return 0

    lax.fori_loop(0, NSH // 2, place, 0)

    left_copy = pltpu.make_async_copy(left, left_out, l_sem)
    left_copy.start()
    out_copies = [None, None]
    height = 2 * width

    def panel(step, slot):
        buf = step % 2
        if out_copies[buf] is not None:
            out_copies[buf].wait()
        ref = coef if slot == 0 else cbuf.at[slot]

        def tile(m, _):
            part = jnp.dot(
                left[pl.ds(pl.multiple_of(m * height, height), height), :],
                ref[...].reshape(NSH * SH, width),
                preferred_element_type=jnp.float32,
            ).astype(jnp.bfloat16)
            stage[buf, pl.ds(m * 2, 2)] = part.reshape(2, width, width)
            return 0

        lax.fori_loop(0, rows // 2, tile, 0)
        copy = pltpu.make_async_copy(stage.at[buf], out.at[step], o_sem.at[buf])
        copy.start()
        out_copies[buf] = copy

    panel(0, FIRST[0])
    c_copies["s"].wait_recv()
    panel(1, FIRST[1])
    c_copies["dh"].wait_recv()
    c_copies["dl"].wait_recv()
    c_copies["sd"] = send_coef(cbuf.at[6], 7, pl.ds(0, NSH), 9, sibling)
    panel(2, FIRST[2])
    panel(3, FIRST[3])
    for name in ("sx", "sy", "sd"):
        c_copies[name].wait_recv()
    coef_copies = [pltpu.make_async_copy(cbuf.at[slot], coefs_out.at[n], k_sem.at[n]) for n, slot in enumerate(SECOND)]
    for copy in coef_copies:
        copy.start()
    for copy in c_copies.values():
        copy.wait_send()
    for copy in coef_copies + out_copies + [left_copy]:
        copy.wait()


def fused_body(pair_ints, shell_pairs, occ_lam, occ_sig, coef_act, slabs):
    width = coef_act.shape[1]
    blocks = shell_pairs.shape[0]
    me = lax.axis_index("mo").astype(jnp.int32)
    here = me.reshape(1)
    rows = 2 * NI
    vmem = pl.BlockSpec(memory_space=pltpu.VMEM)
    smem = pl.BlockSpec(memory_space=pltpu.SMEM)
    hbm = pl.BlockSpec(memory_space=pl.ANY)
    terms, last, pair_coef = pl.pallas_call(
        prepare_kernel,
        out_shape=(
            jax.ShapeDtypeStruct((3, 2 * blocks), jnp.int32),
            jax.ShapeDtypeStruct((2, NSH), jnp.int32),
            jax.ShapeDtypeStruct((4 * rows, KL * KS), jnp.bfloat16),
        ),
        in_specs=[smem, smem, vmem, vmem, vmem],
        out_specs=(vmem, vmem, vmem),
    )(slabs, here, shell_pairs.T, occ_lam, occ_sig.T)
    half = jnp.einsum(
        "mnw,jrw->jmrn", pair_ints.reshape(SH, SH, KL * KS), pair_coef.reshape(4, rows, KL * KS),
        preferred_element_type=jnp.float32,
    ).astype(jnp.bfloat16).reshape(4, SH, rows * SH)
    coef = coef_act.reshape(NSH, SH, width)
    dma = pltpu.SemaphoreType.DMA
    left, coefs, done = pl.pallas_call(
        fused_kernel,
        out_shape=(
            jax.ShapeDtypeStruct((rows * width, NSH * SH), jnp.bfloat16),
            jax.ShapeDtypeStruct((4, NSH, SH, width), jnp.bfloat16),
            jax.ShapeDtypeStruct((4, rows, width, width), jnp.bfloat16),
        ),
        in_specs=[smem, smem, vmem, vmem],
        out_specs=(hbm, hbm, hbm),
        scratch_shapes=[
            pltpu.VMEM((2 * blocks, SH, rows * SH), jnp.bfloat16),
            pltpu.VMEM((8, NSH, SH, width), jnp.bfloat16),
            pltpu.VMEM((NSH, width, SH), jnp.bfloat16),
            pltpu.VMEM((width, rows * SH), jnp.float32),
            pltpu.VMEM((2 * blocks, width, rows * SH), jnp.bfloat16),
            pltpu.VMEM((rows * width, NSH * SH), jnp.bfloat16),
            pltpu.VMEM((2, rows, width, width), jnp.bfloat16),
            dma((3,)), dma((3,)), dma((7,)), dma((7,)), dma((12,)), dma((12,)), dma((2,)),
            dma, dma((4,)),
        ],
        compiler_params=pltpu.CompilerParams(
            collective_id=0, has_side_effects=True, vmem_limit_bytes=56 * 2 ** 20
        ),
        cost_estimate=pl.CostEstimate(
            flops=rows * width * ACT * ACT, bytes_accessed=12 * 2 ** 20, transcendentals=0
        ),
    )(terms, last, half, coef)
    result = pl.pallas_call(
        rest_kernel,
        out_shape=jax.ShapeDtypeStruct((rows, width, ACT), jnp.bfloat16),
        in_specs=[smem, hbm, hbm, hbm],
        out_specs=hbm,
        scratch_shapes=[
            pltpu.VMEM((rows // 2, 2 * width, NSH * SH), jnp.bfloat16),
            pltpu.VMEM((4, NSH * SH, width), jnp.bfloat16),
            pltpu.VMEM((4, rows, width, width), jnp.bfloat16),
            pltpu.VMEM((rows // 2, 4, 2, width, width), jnp.bfloat16),
            dma((rows // 2,)), dma((4,)), dma((4,)), dma((4,)), dma((rows // 2, 4)),
        ],
        compiler_params=pltpu.CompilerParams(vmem_limit_bytes=56 * 2 ** 20),
        cost_estimate=pl.CostEstimate(
            flops=rows * width * ACT * ACT, bytes_accessed=24 * 2 ** 20, transcendentals=0
        ),
    )(here, left, coefs.reshape(4, NSH * SH, width), done)
    return result.reshape(2, 1, NI, width, ACT)


def ket_transform(pair_ints, occ_lam, occ_sig, slab_index):
    blocks_here = pair_ints.shape[0]
    nj_all = occ_sig.shape[1]
    pair_coef = pair_coefficients(occ_lam, occ_sig, slab_index).reshape(nj_all * NI, KL * KS)
    half_ints = jnp.einsum("bqw,xw->bxq", pair_ints, pair_coef, preferred_element_type=jnp.float32)
    return half_ints.astype(jnp.bfloat16).reshape(blocks_here, nj_all, NI, SH * SH)


def remap_pairs(stacked):
    owned = lax.all_to_all(stacked, "ao", split_axis=2, concat_axis=1, tiled=True)
    return lax.all_gather(owned, "mo", axis=1, tiled=True)


def general_body(pair_ints, shell_pairs, occ_lam, occ_sig, coef_act, slabs):
    ao_count = lax.axis_size("ao")
    mo_count = lax.axis_size("mo")
    blocks_here = pair_ints.shape[0]
    panel_width = coef_act.shape[1]
    ao_width = coef_act.shape[0]
    ordered_pairs = (
        shell_pairs.reshape(ao_count, mo_count, blocks_here, 2).transpose(1, 0, 2, 3).reshape(-1, 2)
    )
    halves = [ket_transform(pair_ints, occ_lam, occ_sig, slabs[k]) for k in range(2)]
    gathered_slabs = [remap_pairs(single[None])[0] for single in halves]
    coef_shells = coef_act.reshape(NSH, SH, panel_width)
    coef_all = lax.all_gather(coef_act, "mo", axis=1, tiled=True)

    def bra_transform(gathered):
        block_count = gathered.shape[0]
        pair_rows = gathered.shape[1] * gathered.shape[2]
        blocks = gathered.reshape(block_count, pair_rows, SH, SH)

        def accumulate(running, item):
            values, pair = item
            term_one = jnp.einsum(
                "rmn,ma->ran", values, coef_shells[pair[0]], preferred_element_type=jnp.float32
            )
            term_two = jnp.einsum(
                "rmn,na->ram", values, coef_shells[pair[1]], preferred_element_type=jnp.float32
            ) * (pair[0] != pair[1]).astype(jnp.float32)
            running = running.at[pair[1]].add(term_one)
            return running.at[pair[0]].add(term_two), None

        start_terms = jnp.zeros((NSH, pair_rows, panel_width, SH), jnp.float32)
        left_terms = lax.scan(accumulate, start_terms, (blocks, ordered_pairs))[0]
        left_rounded = left_terms.astype(jnp.bfloat16).transpose(1, 2, 0, 3)
        product = jnp.dot(
            left_rounded.reshape(pair_rows * panel_width, ao_width), coef_all, preferred_element_type=jnp.float32
        )
        return product.astype(jnp.bfloat16).reshape(gathered.shape[1], NI, panel_width, ACT)

    return jnp.stack([bra_transform(gathered) for gathered in gathered_slabs])


def solution(mesh):
    fits = mesh.shape["ao"] == 4 and mesh.shape["mo"] == 8
    return jax.shard_map(
        fused_body if fits else general_body,
        mesh=mesh,
        in_specs=(P(("ao", "mo"), None, None), P(), P(), P(), P(None, "mo"), P()),
        out_specs=P(None, "ao", None, "mo", None),
        check_vma=False,
    )
```
